512 devices in a mesh: gx: 16 (over x_lo, z), gy: 32 (over y, x_hi, core).
Axes of the slice: x: 4 (x_hi: 2, x_lo: 2; x = x_hi * 2 + x_lo), y: 8, z: 8, core: 2. Of those that a mesh axis runs over, the one named last changes fastest.
Arguments:
- features_in: bfloat16 [16, 32, 12, 128, 128], P('gx', 'gy'), may hold values from -6 to 6
- pre_act: bfloat16 [16, 32, 12, 128, 128], P('gx', 'gy'), may hold values from -6 to 6
- cotangent: bfloat16 [16, 32, 12, 128, 128], P('gx', 'gy'), may hold values from -6 to 6
- w_first: bfloat16 [27, 128, 128], replicated, may hold values from -0.375 to 0.375
- w_second: bfloat16 [27, 128, 128], replicated, may hold values from -0.375 to 0.375
- in_slots: int32 [16, 32, 27, 7], P('gx', 'gy'), may hold values from 0 to 28, as said below
- out_slots: int32 [16, 32, 27, 7], P('gx', 'gy'), may hold values from 0 to 12, as said below
- send_lists: int32 [16, 32, 8, 2], P('gx', 'gy'), may hold values from 0 to 11, as said below
Outputs:
- input_grad: bfloat16 [16, 32, 12, 128, 128], P('gx', 'gy')
- weight_grads: float32 [6912, 128], P('gy', 'gx')
The draws below stay inside these ranges and needn't reach their ends.
Inputs may be any that keep to these rules, and one draw needn't show every extreme that they name: `in_slots`: for each device and offset the used entries come first and are distinct slots of the extended blocks; the remaining entries equal 28, the zero block. Every device has some offset with all 7 entries used. `out_slots`: an entry is used exactly where the same entry of in_slots is; used entries of one offset are distinct local blocks, unused ones equal 12. `send_lists`: every device lists exactly 2 distinct local blocks for each heading, also at the grid's edge where nobody receives them.
All inputs are finite; a program needn't handle non-finite values.
Results may differ from the reference program's by a relative error of at most 0.0058.
Values may be sent and summed in bfloat16 or wider, within the bound.
A program may use at most 128 MiB of HBM per device.

```python
import math
import jax
import jax.numpy as jnp
from jax import lax

C = 128
KERNEL = 27
BLOCK = 128
BLOCKS_DEV = 12
MAP_CAP = 7
SEND_CAP = 2
HALO = 16
GRAD_NORM = 458752
N_GX = 16
N_GY = 32


def slot_counts(key):
    level_key, count_key, full_key = jax.random.split(key, 3)
    density = jax.random.randint(level_key, (N_GX, N_GY, 1), 0, 3)
    counts = jax.random.randint(count_key, (N_GX, N_GY, KERNEL), 1, MAP_CAP + 1)
    counts = jnp.where(density == 0, (counts + 2) // 3, counts)
    fullest = jax.random.randint(full_key, (N_GX, N_GY, 1), 0, KERNEL)
    offsets = jnp.arange(KERNEL)[None, None, :]
    return jnp.where(offsets == fullest, MAP_CAP, counts)


def first_of_shuffles(key, groups, extent, keep_count):
    key_list = jax.random.split(key, N_GX * N_GY * groups)
    shuffled = jax.vmap(lambda single: jax.random.permutation(single, extent)[:keep_count])(key_list)
    return shuffled.reshape(N_GX, N_GY, groups, keep_count)


def draw_in_slots(key, part):
    counts = slot_counts(key)
    key = jax.random.fold_in(key, 5)
    chosen = first_of_shuffles(key, KERNEL, BLOCKS_DEV + HALO, MAP_CAP)
    column = jnp.arange(MAP_CAP)[None, None, None, :]
    return jnp.where(column < counts[..., None], chosen, BLOCKS_DEV + HALO).astype(jnp.int32)


def draw_out_slots(key, part):
    counts = slot_counts(key)
    key = jax.random.fold_in(key, 7)
    chosen = first_of_shuffles(key, KERNEL, BLOCKS_DEV, MAP_CAP)
    column = jnp.arange(MAP_CAP)[None, None, None, :]
    return jnp.where(column < counts[..., None], chosen, BLOCKS_DEV).astype(jnp.int32)


def draw_send_lists(key, part):
    key = jax.random.fold_in(key, 9)
    return first_of_shuffles(key, 8, BLOCKS_DEV, SEND_CAP).astype(jnp.int32)


def block_levels(rng, dims, cuts, least, high):
    gain = 1.0
    for position, parts in cuts:
        draws = jax.random.uniform(jax.random.fold_in(jax.random.fold_in(rng, 6), position), (parts,), jnp.float32, least / len(cuts), high / len(cuts))
        gain = gain * jnp.repeat(jnp.exp(draws), dims[position] // parts).reshape((-1,) + (1,) * (len(dims) - 1 - position))
    return gain


def noise(rng, dims, deviation, reach, cuts=(), dtype=jnp.bfloat16):
    array = deviation * jax.random.normal(rng, dims, jnp.float32)
    if cuts:
        array = array * block_levels(rng, dims, cuts, -0.22, 0.18)
    return jnp.clip(array, -reach, reach).astype(dtype)


def setup_inputs(seed: int = 0) -> dict:
    splits = jax.random.split(jax.random.key(seed), 9)
    features_in = noise(splits[0], (N_GX, N_GY, BLOCKS_DEV, BLOCK, C), 1.0, 6.0, ((0, 16), (1, 32)))
    pre_act = noise(splits[1], (N_GX, N_GY, BLOCKS_DEV, BLOCK, C), 1.0, 6.0, ((0, 16), (1, 32)))
    cotangent = noise(splits[2], (N_GX, N_GY, BLOCKS_DEV, BLOCK, C), 1.0, 6.0, ((0, 16), (1, 32)))
    w_first = noise(splits[3], (KERNEL, C, C), (2 * C) ** -0.5, 0.375)
    w_second = noise(splits[4], (KERNEL, C, C), (2 * C) ** -0.5, 0.375)
    in_slots = draw_in_slots(jax.random.fold_in(splits[8], 71), 0)
    out_slots = draw_out_slots(jax.random.fold_in(splits[8], 71), 0)
    send_lists = draw_send_lists(jax.random.fold_in(splits[8], 71), 0)
    return dict(features_in=features_in, pre_act=pre_act, cotangent=cotangent, w_first=w_first, w_second=w_second, in_slots=in_slots, out_slots=out_slots, send_lists=send_lists)


HEADINGS = ((-1, -1), (-1, 0), (-1, 1), (0, -1), (0, 1), (1, -1), (1, 0), (1, 1))

def displaced(layout, step_x, step_y):
    widths = ((1, 1), (1, 1)) + ((0, 0),) * (layout.ndim - 2)
    padded = jnp.pad(layout, widths)
    return padded[1 - step_x:1 - step_x + N_GX, 1 - step_y:1 - step_y + N_GY]

def halo_blocks(layout, send_lists):
    arrived = []
    for heading in range(8):
        index_rows = jnp.broadcast_to(send_lists[:, :, heading, :, None, None], (N_GX, N_GY, SEND_CAP, BLOCK, C))
        chosen = jnp.take_along_axis(layout, index_rows, axis=2)
        arrived.append(displaced(chosen, HEADINGS[heading][0], HEADINGS[heading][1]))
    return jnp.concatenate(arrived, axis=2)

def returned_blocks(halo_part):
    arrived = []
    for heading in range(8):
        offset_start = heading * SEND_CAP
        arrived.append(displaced(halo_part[:, :, offset_start:offset_start + SEND_CAP], -HEADINGS[heading][0], -HEADINGS[heading][1]))
    return jnp.concatenate(arrived, axis=2)

def offsets_back(source_ext, grad_ext, weight, slot_in, slot_out):
    channels = source_ext.shape[-1]

    def per_offset(running, inputs):
        offset_weight, in_row, out_row = inputs
        sources = source_ext[in_row].reshape(-1, channels)
        grad_rows = grad_ext[out_row].reshape(-1, channels)
        weight_grad = lax.dot_general(sources, grad_rows, (((0,), (0,)), ((), ())), preferred_element_type=jnp.float32)
        back_rows = lax.dot_general(grad_rows, offset_weight, (((1,), (1,)), ((), ())), preferred_element_type=jnp.float32)
        running = running.at[in_row].add(back_rows.reshape((in_row.shape[0],) + source_ext.shape[1:]))
        return (running, weight_grad)
    zeros_block = jnp.zeros(source_ext.shape, jnp.float32)
    return lax.scan(per_offset, zeros_block, (weight, slot_in, slot_out))

def add_returned(own_part, returned, send_rows):
    return own_part.at[send_rows.reshape(-1)].add(returned.astype(jnp.float32))

def layer_pass(source_ext, grad_ext, weight, in_slots, out_slots, activate):
    devices = N_GX * N_GY
    source_flat = source_ext.reshape((devices,) + source_ext.shape[2:])
    grad_flat = grad_ext.reshape((devices,) + grad_ext.shape[2:])
    in_flat = in_slots.reshape(devices, KERNEL, MAP_CAP)
    out_flat = out_slots.reshape(devices, KERNEL, MAP_CAP)

    def per_device(running, inputs):
        source_dev, grad_dev, in_dev, out_dev = inputs
        if activate:
            source_dev = jax.nn.silu(source_dev.astype(jnp.float32)).astype(jnp.bfloat16)
        partial_value, weight_grad = offsets_back(source_dev, grad_dev, weight, in_dev, out_dev)
        own_part = partial_value[:BLOCKS_DEV]
        halo_part = partial_value[BLOCKS_DEV:BLOCKS_DEV + HALO].astype(jnp.bfloat16)
        return (running + weight_grad, (own_part, halo_part))
    start = jnp.zeros((KERNEL, C, C), jnp.float32)
    weight_sum, (own_parts, halo_parts) = lax.scan(per_device, start, (source_flat, grad_flat, in_flat, out_flat))
    return (weight_sum, own_parts, halo_parts)

def gather_back(own_parts, halo_parts, send_lists):
    devices = N_GX * N_GY
    halo_grid = halo_parts.reshape((N_GX, N_GY) + halo_parts.shape[1:])
    returned = returned_blocks(halo_grid).reshape((devices,) + halo_parts.shape[1:])
    send_flat = send_lists.reshape(devices, 8 * SEND_CAP)
    summed = jax.vmap(add_returned)(own_parts, returned, send_flat)
    return summed.reshape((N_GX, N_GY) + own_parts.shape[1:])

def reference(features_in, pre_act, cotangent, w_first, w_second, in_slots, out_slots, send_lists):
    padding = jnp.zeros((N_GX, N_GY, 1, BLOCK, C), jnp.bfloat16)
    pre_ext = jnp.concatenate([pre_act, halo_blocks(pre_act, send_lists), padding], axis=2)
    grad_ext = jnp.concatenate([cotangent, padding], axis=2)
    second_weight, own_second, halo_second = layer_pass(pre_ext, grad_ext, w_second, in_slots, out_slots, True)
    act_grad = gather_back(own_second, halo_second, send_lists)
    pre_value = pre_act.astype(jnp.float32)
    sigmoid_value = jax.nn.sigmoid(pre_value)
    silu_slope = sigmoid_value * (1.0 + pre_value * (1.0 - sigmoid_value))
    pre_grad = (act_grad * silu_slope).astype(jnp.bfloat16)
    feat_ext = jnp.concatenate([features_in, halo_blocks(features_in, send_lists), padding], axis=2)
    pre_grad_ext = jnp.concatenate([pre_grad, padding], axis=2)
    first_weight, own_first, halo_first = layer_pass(feat_ext, pre_grad_ext, w_first, in_slots, out_slots, False)
    input_grad = gather_back(own_first, halo_first, send_lists).astype(jnp.bfloat16)
    weight_grads = jnp.concatenate([first_weight, second_weight], axis=0).reshape(2 * KERNEL * C, C)
    weight_grads = weight_grads * (1.0 / math.sqrt(GRAD_NORM))
    return (input_grad, weight_grads)
```

```python
import functools
import math

import jax
import jax.numpy as jnp
from jax import lax
from jax.experimental import pallas as pl
from jax.experimental.pallas import tpu as pltpu
from jax.sharding import PartitionSpec as P

HEADINGS = ((-1, -1), (-1, 0), (-1, 1), (0, -1), (0, 1), (1, -1), (1, 0), (1, 1))
KERNEL, MAP_CAP, BLOCKS, SEND_CAP, BLOCK = 27, 7, 12, 2, 128
HALO = 8 * SEND_CAP
ZERO = BLOCKS + HALO
SIDE = 14
MESH = pl.DeviceIdType.MESH
F32, BF16 = jnp.float32, jnp.bfloat16

T_IN = 0
T_OUT = T_IN + KERNEL * MAP_CAP
T_INV = T_OUT + KERNEL * MAP_CAP
T_BACK = T_INV + KERNEL * ZERO
T_SEND = T_BACK + 8 * BLOCKS
T_END = T_SEND + HALO


class Grid:
    def __init__(self, n_gx, n_gy, x_lo, x_hi):
        self.n_gx, self.n_gy, self.x_lo, self.x_hi = n_gx, n_gy, x_lo, x_hi
        self.z = n_gx // x_lo
        self.y = n_gy // (2 * x_hi)
        self.chips = n_gy // 2
        self.columns = 128 // n_gx
        self.rows = 2 * KERNEL * 128 // n_gy
        self.rows_pad = -(-self.rows // 256) * 256
        self.half = n_gy // 2
        self.quarter = n_gy // 4
        self.z_rows = 128 // self.z
        self.sources = x_lo * self.chips


def sigmoid(value):
    return 1.0 / (1.0 + jnp.exp(-value))


def kernel(grid, tab, feat, pre, cot, w1, w2, grad_out, weight_out, act_own, act_ext, feat_ext, g_ext, pg_ext,
           gt, acc, sb_act, sb_feat, sb_g, rb_g1, rb_g2, core_send, core_recv, own, z_send, z_recv, line,
           f_send, f_recv, halo_ssem, halo_rsem, core_ssem, core_rsem, z_ssem, z_rsem, f_ssem, f_rsem):
    gd = grid
    p, q = lax.axis_index("gx"), lax.axis_index("gy")
    z, xl = p % gd.z, p // gd.z
    core, chip_q = q % 2, q // 2

    barrier = pltpu.get_barrier_semaphore()

    def hello(px, qy):
        pl.semaphore_signal(barrier, inc=1, device_id=(px, qy), device_id_type=MESH)

    def hello_q(d, _):
        hello(p, (q + d) % gd.n_gy)
        return 0

    lax.fori_loop(1, gd.n_gy, hello_q, 0)
    greeted = gd.n_gy - 1
    for dx in range(1, gd.x_lo):
        other = ((xl + dx) % gd.x_lo) * gd.z + z

        def hello_x(d, _):
            hello(other, (q + d) % gd.n_gy)
            return 0

        lax.fori_loop(0, gd.n_gy, hello_x, 0)
        greeted += gd.n_gy
    for dz in range(1, gd.z):
        hello(xl * gd.z + (z + dz) % gd.z, q)
        greeted += 1
    for a, b in HEADINGS:
        if a != 0:
            hello((p + a + gd.n_gx) % gd.n_gx, (q + b + gd.n_gy) % gd.n_gy)
            greeted += 1

    zero_block = jnp.zeros((BLOCK, 128), BF16)
    act_ext[ZERO] = zero_block
    feat_ext[ZERO] = zero_block
    g_ext[BLOCKS] = zero_block
    pg_ext[BLOCKS] = zero_block
    gt[BLOCKS] = zero_block
    returned = (rb_g1, rb_g2)
    for buffer in returned:
        buffer[HALO] = zero_block

    def load_own(b, _):
        value = pre[b].astype(F32)
        value = (value * sigmoid(value)).astype(BF16)
        act_own[b] = value
        act_ext[b] = value
        feat_ext[b] = feat[b]
        g_ext[b] = cot[b]
        return 0

    lax.fori_loop(0, BLOCKS, load_own, 0)

    def pick(i, _):
        sb_act[i] = act_own[tab[T_SEND + i]]
        sb_feat[i] = feat[tab[T_SEND + i]]
        return 0

    lax.fori_loop(0, HALO, pick, 0)
    pl.semaphore_wait(barrier, greeted)

    def halo_copy(kind, e, src, dst, a, b):
        return pltpu.make_async_remote_copy(
            src_ref=src, dst_ref=dst, send_sem=halo_ssem.at[kind, e], recv_sem=halo_rsem.at[kind, e],
            device_id=((p + a + gd.n_gx) % gd.n_gx, (q + b + gd.n_gy) % gd.n_gy), device_id_type=MESH)

    def forth(kind, src, ext):
        return [halo_copy(kind, e, src.at[pl.ds(2 * e, 2)], ext.at[pl.ds(BLOCKS + 2 * e, 2)], a, b)
                for e, (a, b) in enumerate(HEADINGS)]

    def back(kind, layer):
        return [halo_copy(kind, e, sb_g.at[layer, pl.ds(2 * e, 2)], returned[layer].at[pl.ds(2 * e, 2)], -a, -b)
                for e, (a, b) in enumerate(HEADINGS)]

    def start(copies):
        for copy in copies:
            copy.start()

    def arrive(copies):
        for copy in copies:
            copy.wait_recv()

    act_copies, feat_copies = forth(0, sb_act, act_ext), forth(1, sb_feat, feat_ext)
    back_copies = [back(3, 0), back(2, 1)]
    start(act_copies)

    def products(grads, weight, j, n):
        lhs = jnp.concatenate(
            [jnp.concatenate([grads[tab[T_INV + k * ZERO + j + t]] for k in range(KERNEL)], axis=1)
             for t in range(n)], axis=0)
        rhs = jnp.concatenate([weight[k] for k in range(KERNEL)], axis=1)
        out = lax.dot_general(lhs, rhs, (((1,), (1,)), ((), ())), preferred_element_type=F32)
        return out.reshape(n, BLOCK, 128)

    def halo_partial(grads, weight, layer):
        def group(i, _):
            sb_g[layer, pl.ds(4 * i, 4)] = products(grads, weight, BLOCKS + 4 * i, 4).astype(BF16)
            return 0

        lax.fori_loop(0, HALO // 4, group, 0)

    def own_partial(grads, weight):
        def group(i, _):
            acc[pl.ds(4 * i, 4)] = products(grads, weight, 4 * i, 4)
            return 0

        lax.fori_loop(0, BLOCKS // 4, group, 0)

    def with_returned(b, layer):
        total = acc[b]
        for e in range(8):
            total = total + returned[layer][tab[T_BACK + e * BLOCKS + b]].astype(F32)
        return total

    def turn(grads):
        def one(b, _):
            t = grads[b].astype(F32).T
            step = gd.z * gd.columns
            t = jnp.concatenate(
                [t[x * step + c * gd.columns:x * step + (c + 1) * gd.columns]
                 for c in range(gd.z) for x in range(gd.x_lo)], axis=0)
            gt[b] = t.astype(BF16)
            return 0

        lax.fori_loop(0, BLOCKS, one, 0)

    def weight_term(sources, k):
        lhs = jnp.concatenate([gt[tab[T_OUT + k * MAP_CAP + m]] for m in range(MAP_CAP)], axis=1)
        rhs = jnp.concatenate([sources[tab[T_IN + k * MAP_CAP + m]] for m in range(MAP_CAP)], axis=0)
        return lax.dot_general(lhs, rhs, (((1,), (0,)), ((), ())), preferred_element_type=F32)

    def core_copy(layer):
        return pltpu.make_async_remote_copy(
            src_ref=core_send.at[layer], dst_ref=core_recv.at[layer], send_sem=core_ssem.at[layer],
            recv_sem=core_rsem.at[layer], device_id=(p, q + 1 - 2 * core), device_id_type=MESH)

    first_k = core * (KERNEL - SIDE)
    other_k = (1 - core) * (KERNEL - SIDE)
    core_copies = [core_copy(0), core_copy(1)]

    def weight_terms(sources, layer):
        def other(i, _):
            for u in range(7):
                core_send[layer, 7 * i + u] = weight_term(sources, other_k + 7 * i + u).astype(BF16)
            return 0

        lax.fori_loop(0, SIDE // 7, other, 0)
        core_copies[layer].start()

        def mine(i, _):
            for u in range(7):
                own[7 * i + u] = weight_term(sources, first_k + 7 * i + u)
            return 0

        lax.fori_loop(0, SIDE // 7, mine, 0)

    def z_copy(layer, dz):
        there = (z + dz) % gd.z
        return pltpu.make_async_remote_copy(
            src_ref=z_send.at[layer, there], dst_ref=z_recv.at[layer, dz], send_sem=z_ssem.at[layer, dz],
            recv_sem=z_rsem.at[layer, dz], device_id=(xl * gd.z + there, q), device_id_type=MESH)

    z_copies = [[z_copy(layer, dz) for dz in range(1, gd.z)] for layer in range(2)]

    def to_z(layer):
        core_copies[layer].wait_recv()

        def one(i, _):
            total = own[i] + core_recv[layer, i].astype(F32)
            total = total.astype(BF16)
            for c in range(gd.z):
                z_send[layer, c, i] = total[c * gd.z_rows:(c + 1) * gd.z_rows]
            return 0

        lax.fori_loop(0, SIDE, one, 0)
        start(z_copies[layer])

    source = xl * gd.chips + chip_q

    def f_copy(layer, slot, target):
        return pltpu.make_async_remote_copy(
            src_ref=f_send.at[layer, slot], dst_ref=f_recv.at[source], send_sem=f_ssem.at[layer, slot],
            recv_sem=f_rsem.at[source], device_id=target, device_id_type=MESH)

    def f_targets(layer):
        for x in range(gd.x_lo):
            for i in range(gd.quarter):
                target = (x * gd.z + z, layer * gd.half + core * gd.quarter + i)
                away = jnp.logical_or(target[0] != p, target[1] != q)
                yield x, i, x * gd.quarter + i, target, away

    def to_holders(layer):
        arrive(z_copies[layer])

        def one(i, _):
            total = z_send[layer, z, i].astype(F32)
            for dz in range(1, gd.z):
                total = total + z_recv[layer, dz, i].astype(F32)
            line[i] = total
            return 0

        lax.fori_loop(0, SIDE, one, 0)
        whole = jnp.concatenate([line[i] for i in range(SIDE)], axis=1)
        width = SIDE * 128
        shift = gd.rows * gd.quarter - (KERNEL - SIDE) * 128
        whole = jnp.where(core == 0, whole, pltpu.roll(whole, (width - shift) % width, 1))
        for i in range(gd.quarter):
            begin = i * gd.rows
            part = whole if begin == 0 else pltpu.roll(whole, width - begin, 1)
            part = part[:, :gd.rows_pad]
            half = gd.rows_pad // 2
            for x in range(gd.x_lo):
                chunk = part[x * gd.columns:(x + 1) * gd.columns]
                chunk = jnp.concatenate([chunk[:, :half], chunk[:, half:]], axis=0).astype(BF16)
                f_send[layer, x * gd.quarter + i] = chunk
        for x, i, slot, target, away in f_targets(layer):
            @pl.when(away)
            def _():
                f_copy(layer, slot, target).start()

            @pl.when(jnp.logical_not(away))
            def _():
                f_recv[source] = f_send[layer, slot]

    turn(g_ext)
    halo_partial(g_ext, w2, 1)
    start(back_copies[1])
    start(feat_copies)
    own_partial(g_ext, w2)
    arrive(act_copies)
    weight_terms(act_ext, 1)
    to_z(1)
    arrive(back_copies[1])

    def slope(b, _):
        value = pre[b].astype(F32)
        gate = sigmoid(value)
        pg_ext[b] = (with_returned(b, 1) * (gate * (1.0 + value * (1.0 - gate)))).astype(BF16)
        return 0

    lax.fori_loop(0, BLOCKS, slope, 0)
    turn(pg_ext)
    arrive(feat_copies)
    weight_terms(feat_ext, 0)
    to_z(0)
    halo_partial(pg_ext, w1, 0)
    start(back_copies[0])
    to_holders(1)
    own_partial(pg_ext, w1)
    to_holders(0)
    arrive(back_copies[0])

    def finish(b, _):
        grad_out[b] = with_returned(b, 0).astype(BF16)
        return 0

    lax.fori_loop(0, BLOCKS, finish, 0)

    sender_core = (q % gd.half) // gd.quarter

    def others(s, _):
        @pl.when(jnp.logical_not(jnp.logical_and(s == source, sender_core == core)))
        def _():
            pltpu.make_async_remote_copy(
                src_ref=f_send.at[0, 0], dst_ref=f_recv.at[s], send_sem=f_ssem.at[0, 0],
                recv_sem=f_rsem.at[s], device_id=(p, q + 1 - 2 * core), device_id_type=MESH).wait_recv()
        return 0

    lax.fori_loop(0, gd.sources, others, 0)
    total = f_recv[0].astype(F32)
    for s in range(1, gd.sources):
        total = total + f_recv[s].astype(F32)
    total = total * (1.0 / math.sqrt(MAP_CAP * BLOCK * gd.n_gx * gd.n_gy))
    total = jnp.concatenate([total[:gd.columns], total[gd.columns:]], axis=1)
    if gd.columns < 128:
        total = jnp.concatenate([total, jnp.zeros((128 - gd.columns, gd.rows_pad), F32)], axis=0)
    weight_out[...] = total.T[:gd.rows, :gd.columns]

    for copies in (act_copies, feat_copies, back_copies[0], back_copies[1], core_copies, z_copies[0], z_copies[1]):
        for copy in copies:
            copy.wait_send()
    for layer in range(2):
        for x, i, slot, target, away in f_targets(layer):
            @pl.when(away)
            def _():
                f_copy(layer, slot, target).wait_send()


def index_tables(grid, in_slots, out_slots, send_lists):
    p, q = lax.axis_index("gx"), lax.axis_index("gy")
    a = jnp.array([h[0] for h in HEADINGS], jnp.int32)
    b = jnp.array([h[1] for h in HEADINGS], jnp.int32)

    def inside(x, y):
        return (x >= 0) & (x < grid.n_gx) & (y >= 0) & (y < grid.n_gy)

    comes = inside(p - a, q - b)
    slot_heading = (in_slots - BLOCKS) // SEND_CAP
    missing = jnp.any((slot_heading[..., None] == jnp.arange(8)) & (in_slots[..., None] >= BLOCKS) & ~comes, axis=-1)
    read_slots = jnp.where(missing, ZERO, in_slots)
    slots = jnp.arange(ZERO, dtype=jnp.int32)
    inverse = jnp.min(jnp.where(in_slots[:, :, None] == slots, out_slots[:, :, None], BLOCKS), axis=1)
    returns = inside(p + a, q + b)
    own_blocks = jnp.arange(BLOCKS, dtype=jnp.int32)
    place = 2 * jnp.arange(8, dtype=jnp.int32)[:, None] + jnp.arange(SEND_CAP, dtype=jnp.int32)
    hit = (send_lists[:, :, None] == own_blocks) & returns[:, None, None]
    returned = jnp.min(jnp.where(hit, place[:, :, None], HALO), axis=1)
    parts = [read_slots, out_slots, inverse, returned, send_lists]
    return jnp.concatenate([part.reshape(-1) for part in parts])


def per_device(grid, features_in, pre_act, cotangent, w_first, w_second, in_slots, out_slots, send_lists):
    gd = grid
    table = index_tables(gd, in_slots[0, 0], out_slots[0, 0], send_lists[0, 0])
    ext = ZERO + 1
    half = gd.rows_pad // 2
    dma = pltpu.SemaphoreType.DMA
    block = (BLOCK, 128)
    vmem = pl.BlockSpec(memory_space=pltpu.VMEM)
    flops = 2 * 128 ** 3 * KERNEL * 2 * (ZERO + MAP_CAP)
    grad, weight = pl.pallas_call(
        functools.partial(kernel, gd),
        out_shape=(
            jax.ShapeDtypeStruct((BLOCKS,) + block, BF16),
            jax.ShapeDtypeStruct((gd.rows, gd.columns), F32),
        ),
        in_specs=[pl.BlockSpec(memory_space=pltpu.SMEM)] + [vmem] * 5,
        out_specs=(vmem, vmem),
        scratch_shapes=[
            pltpu.VMEM((BLOCKS,) + block, BF16),
            pltpu.VMEM((ext,) + block, BF16),
            pltpu.VMEM((ext,) + block, BF16),
            pltpu.VMEM((BLOCKS + 1,) + block, BF16),
            pltpu.VMEM((BLOCKS + 1,) + block, BF16),
            pltpu.VMEM((BLOCKS + 1,) + block, BF16),
            pltpu.VMEM((BLOCKS,) + block, F32),
            pltpu.VMEM((HALO,) + block, BF16),
            pltpu.VMEM((HALO,) + block, BF16),
            pltpu.VMEM((2, HALO) + block, BF16),
            pltpu.VMEM((HALO + 1,) + block, BF16),
            pltpu.VMEM((HALO + 1,) + block, BF16),
            pltpu.VMEM((2, SIDE) + block, BF16),
            pltpu.VMEM((2, SIDE) + block, BF16),
            pltpu.VMEM((SIDE,) + block, F32),
            pltpu.VMEM((2, gd.z, SIDE, gd.z_rows, 128), BF16),
            pltpu.VMEM((2, gd.z, SIDE, gd.z_rows, 128), BF16),
            pltpu.VMEM((SIDE, gd.z_rows, 128), F32),
            pltpu.VMEM((2, gd.x_lo * gd.quarter, 2 * gd.columns, half), BF16),
            pltpu.VMEM((gd.sources, 2 * gd.columns, half), BF16),
            dma((4, 8)),
            dma((4, 8)),
            dma((2,)),
            dma((2,)),
            dma((2, gd.z)),
            dma((2, gd.z)),
            dma((2, gd.x_lo * gd.quarter)),
            dma((gd.sources,)),
        ],
        compiler_params=pltpu.CompilerParams(
            collective_id=0, has_side_effects=True, vmem_limit_bytes=40 * 1024 * 1024
        ),
        cost_estimate=pl.CostEstimate(flops=flops, bytes_accessed=8 * 2 ** 20, transcendentals=0),
    )(table, features_in[0, 0], pre_act[0, 0], cotangent[0, 0], w_first, w_second)
    return grad[None, None], weight


def build(mesh, x_lo, x_hi):
    grid = Grid(mesh.shape["gx"], mesh.shape["gy"], x_lo, x_hi)
    in_specs = (
        P("gx", "gy", None, None, None),
        P("gx", "gy", None, None, None),
        P("gx", "gy", None, None, None),
        P(),
        P(),
        P("gx", "gy", None, None),
        P("gx", "gy", None, None),
        P("gx", "gy", None, None),
    )
    out_specs = (P("gx", "gy", None, None, None), P("gy", "gx"))
    return jax.shard_map(
        functools.partial(per_device, grid), mesh=mesh, in_specs=in_specs, out_specs=out_specs, check_vma=False
    )


def solution(mesh):
    return build(mesh, 2, 2)
```

```python
import functools
import math

import jax
import jax.numpy as jnp
from jax import lax
from jax.experimental import pallas as pl
from jax.experimental.pallas import tpu as pltpu
from jax.sharding import PartitionSpec as P

HEADINGS = ((-1, -1), (-1, 0), (-1, 1), (0, -1), (0, 1), (1, -1), (1, 0), (1, 1))
KERNEL, MAP_CAP, BLOCKS, SEND_CAP, BLOCK = 27, 7, 12, 2, 128
HALO = 8 * SEND_CAP
ZERO = BLOCKS + HALO
SIDE = 14
MESH = pl.DeviceIdType.MESH
F32, BF16 = jnp.float32, jnp.bfloat16

class Grid:
    def __init__(self, n_gx, n_gy, x_lo, x_hi):
        self.n_gx, self.n_gy, self.x_lo, self.x_hi = n_gx, n_gy, x_lo, x_hi
        self.z = n_gx // x_lo
        self.y = n_gy // (2 * x_hi)
        self.chips = n_gy // 2
        self.columns = 128 // n_gx
        self.rows = 2 * KERNEL * 128 // n_gy
        self.rows_pad = -(-self.rows // 256) * 256
        self.half = n_gy // 2
        self.quarter = n_gy // 4
        self.ring = self.z
        self.sources = x_lo * x_hi * self.ring


def sigmoid(value):
    return 1.0 / (1.0 + jnp.exp(-value))


def kernel(grid, in_hbm, out_hbm, send_hbm, feat_hbm, pre_hbm, cot_hbm, w1_hbm, w2_hbm, grad_hbm, weight_out,
           in_vec, out_vec, inv_vec, in_tab, out_tab, send_tab, inv_tab, feat, pre, w1, w2, grad_out,
           act_own, act_ext, feat_ext, g_ext, pg_ext, gt, acc, sb_act, sb_feat, sb_g, rb_g1, rb_g2,
           core_send, core_recv, own, r_send, r_recv, line, f_send, f_recv,
           load_sem, halo_ssem, halo_rsem, core_ssem, core_rsem, r_ssem, r_rsem, f_ssem, f_rsem):
    gd = grid
    p, q = lax.axis_index("gx"), lax.axis_index("gy")
    z, xl = p % gd.z, p // gd.z
    core, chip_q = q % 2, q // 2
    y, xh = chip_q // gd.x_hi, chip_q % gd.x_hi

    def load(n, src, dst):
        copy = pltpu.make_async_copy(src, dst, load_sem.at[n])
        copy.start()
        return copy

    got_in = load(0, in_hbm, in_vec)
    got_out = load(1, out_hbm, out_vec)
    got_send = load(2, send_hbm, send_tab)
    got_pre = load(3, pre_hbm, pre)
    got_feat = load(4, feat_hbm, feat)
    got_cot = load(5, cot_hbm, g_ext.at[pl.ds(0, BLOCKS)])
    got_w2 = load(6, w2_hbm, w2)
    got_in_tab = load(7, in_hbm, in_tab)
    got_out_tab = load(8, out_hbm, out_tab)
    got_feat_ext = load(9, feat_hbm, feat_ext.at[pl.ds(0, BLOCKS)])
    got_w1 = load(10, w1_hbm, w1)

    barrier = pltpu.get_barrier_semaphore()

    def hello(px, qy):
        pl.semaphore_signal(barrier, inc=1, device_id=(px, qy), device_id_type=MESH)

    sender_core = (q % gd.half) // gd.quarter

    def hello_source(s, _):
        x, i = s // gd.ring, s % gd.ring
        px = jnp.where(xl == 0, (x // gd.x_hi) * gd.z + i, (x // gd.x_hi) * gd.z + z)
        qy = (jnp.where(xl == 0, z, i) * gd.x_hi + x % gd.x_hi) * 2 + sender_core
        hello(px, qy)
        return 0

    lax.fori_loop(0, gd.sources, hello_source, 0)
    for d in range(1, gd.ring):
        hello(xl * gd.z + (z + d) % gd.z, q)
        hello(p, (((y + d) % gd.y) * gd.x_hi + xh) * 2 + core)
    hello(p, q + 1 - 2 * core)
    for a, b in HEADINGS:
        hello((p + a + gd.n_gx) % gd.n_gx, (q + b + gd.n_gy) % gd.n_gy)
    greeted = 2 * gd.x_lo * gd.quarter + 2 * (gd.ring - 1) + 1 + 8

    zero_block = jnp.zeros((BLOCK, 128), BF16)
    returned = (rb_g1, rb_g2)
    for buffer, place in ((act_ext, ZERO), (feat_ext, ZERO), (g_ext, BLOCKS), (pg_ext, BLOCKS), (gt, BLOCKS),
                          (rb_g1, HALO), (rb_g2, HALO)):
        buffer[place] = zero_block

    got_in.wait()
    got_out.wait()
    inv_vec[...] = jnp.zeros(inv_vec.shape, jnp.int32)
    slots = lax.broadcasted_iota(jnp.int32, (ZERO, KERNEL), 0)
    inverse = jnp.full((ZERO, KERNEL), BLOCKS, jnp.int32)
    for m in range(MAP_CAP):
        inverse = jnp.where(in_vec[m] == slots, out_vec[m], inverse)
    inv_vec[:ZERO, :KERNEL] = inverse
    got_inv = load(11, inv_vec, inv_tab)

    got_pre.wait()

    def load_own(b, _):
        value = pre[b].astype(F32)
        value = (value * sigmoid(value)).astype(BF16)
        act_own[b] = value
        act_ext[b] = value
        return 0

    lax.fori_loop(0, BLOCKS, load_own, 0)
    got_send.wait()
    got_feat.wait()

    def pick(e, _):
        for s in range(SEND_CAP):
            sb_act[2 * e + s] = act_own[send_tab[s, e]]
            sb_feat[2 * e + s] = feat[send_tab[s, e]]
        return 0

    lax.fori_loop(0, 8, pick, 0)

    def halo_copy(kind, e, src, dst, a, b):
        return pltpu.make_async_remote_copy(
            src_ref=src, dst_ref=dst, send_sem=halo_ssem.at[kind, e], recv_sem=halo_rsem.at[kind, e],
            device_id=((p + a + gd.n_gx) % gd.n_gx, (q + b + gd.n_gy) % gd.n_gy), device_id_type=MESH)

    def forth(kind, src, ext):
        return [halo_copy(kind, e, src.at[pl.ds(2 * e, 2)], ext.at[pl.ds(BLOCKS + 2 * e, 2)], a, b)
                for e, (a, b) in enumerate(HEADINGS)]

    def back(kind, layer):
        return [halo_copy(kind, e, sb_g.at[layer, pl.ds(2 * e, 2)], returned[layer].at[pl.ds(2 * e, 2)], -a, -b)
                for e, (a, b) in enumerate(HEADINGS)]

    def start(copies):
        for copy in copies:
            copy.start()

    def arrive(copies):
        for copy in copies:
            copy.wait_recv()

    def arrive_halo(copies, buffer, first, sign):
        arrive(copies)
        for e, (a, b) in enumerate(HEADINGS):
            px, qy = p + sign * a, q + sign * b
            inside = (px >= 0) & (px < gd.n_gx) & (qy >= 0) & (qy < gd.n_gy)

            @pl.when(jnp.logical_not(inside))
            def _():
                for s in range(SEND_CAP):
                    buffer[first + 2 * e + s] = zero_block

    act_copies, feat_copies = forth(0, sb_act, act_ext), forth(1, sb_feat, feat_ext)
    back_copies = [back(3, 0), back(2, 1)]

    def products(grads, weight, j, n):
        lhs = jnp.concatenate(
            [jnp.concatenate([grads[inv_tab[j + t, k]] for k in range(KERNEL)], axis=1) for t in range(n)], axis=0)
        rhs = jnp.concatenate([weight[k] for k in range(KERNEL)], axis=1)
        out = lax.dot_general(lhs, rhs, (((1,), (1,)), ((), ())), preferred_element_type=F32)
        return out.reshape(n, BLOCK, 128)

    def halo_partial(grads, weight, layer):
        def group(i, _):
            sb_g[layer, pl.ds(4 * i, 4)] = products(grads, weight, BLOCKS + 4 * i, 4).astype(BF16)
            return 0

        lax.fori_loop(0, HALO // 4, group, 0)

    def own_partial(grads, weight):
        def group(i, _):
            acc[pl.ds(4 * i, 4)] = products(grads, weight, 4 * i, 4)
            return 0

        lax.fori_loop(0, BLOCKS // 4, group, 0)

    def with_returned(b, layer):
        total = acc[b]
        for e in range(8):
            place = jnp.where(send_tab[0, e] == b, 2 * e, jnp.where(send_tab[1, e] == b, 2 * e + 1, HALO))
            total = total + returned[layer][place].astype(F32)
        return total

    def turn(grads):
        def one(b, _):
            gt[b] = grads[b].T
            return 0

        lax.fori_loop(0, BLOCKS, one, 0)

    def weight_term(sources, k):
        lhs = jnp.concatenate([gt[out_tab[m, 0, k]] for m in range(MAP_CAP)], axis=1)
        rhs = jnp.concatenate([sources[in_tab[m, 0, k]] for m in range(MAP_CAP)], axis=0)
        return lax.dot_general(lhs, rhs, (((1,), (0,)), ((), ())), preferred_element_type=F32)

    def core_copy(layer):
        return pltpu.make_async_remote_copy(
            src_ref=core_send.at[layer], dst_ref=core_recv.at[layer], send_sem=core_ssem.at[layer],
            recv_sem=core_rsem.at[layer], device_id=(p, q + 1 - 2 * core), device_id_type=MESH)

    first_k = core * (KERNEL - SIDE)
    other_k = (1 - core) * (KERNEL - SIDE)
    core_copies = [core_copy(0), core_copy(1)]

    def weight_terms(sources, layer):
        def other(i, _):
            for u in range(7):
                core_send[layer, 7 * i + u] = weight_term(sources, other_k + 7 * i + u).astype(BF16)
            return 0

        lax.fori_loop(0, SIDE // 7, other, 0)
        core_copies[layer].start()

        def mine(i, _):
            for u in range(7):
                own[7 * i + u] = weight_term(sources, first_k + 7 * i + u)
            return 0

        lax.fori_loop(0, SIDE // 7, mine, 0)

    def ring_copy(layer, x, d):
        if x == 0:
            there = (y + d) % gd.y
            target = (p, (there * gd.x_hi + xh) * 2 + core)
        else:
            there = (z + d) % gd.z
            target = (xl * gd.z + there, q)
        return pltpu.make_async_remote_copy(
            src_ref=r_send.at[layer, x, there], dst_ref=r_recv.at[layer, x, d], send_sem=r_ssem.at[layer, x, d],
            recv_sem=r_rsem.at[layer, x, d], device_id=target, device_id_type=MESH)

    ring_copies = [[[ring_copy(layer, x, d) for d in range(1, gd.ring)] for x in range(gd.x_lo)] for layer in range(2)]

    def to_rings(layer):
        core_copies[layer].wait_recv()

        def one(i, _):
            low = own[i] + core_recv[layer, i].astype(F32)
            high = own[i + SIDE // 2] + core_recv[layer, i + SIDE // 2].astype(F32)
            for x in range(gd.x_lo):
                for c in range(gd.ring):
                    rows = slice((x * gd.ring + c) * gd.columns, (x * gd.ring + c + 1) * gd.columns)
                    r_send[layer, x, c, i] = jnp.concatenate([low[rows], high[rows]], axis=0).astype(BF16)
            return 0

        lax.fori_loop(0, SIDE // 2, one, 0)
        for x in range(gd.x_lo):
            start(ring_copies[layer][x])

    places = [(xl * gd.x_hi + xh) * gd.ring + z, (xl * gd.x_hi + xh) * gd.ring + y]

    def f_copy(layer, x, i):
        column = y if x == 0 else z
        target = (x * gd.z + column, layer * gd.half + core * gd.quarter + i)
        slot = x * gd.quarter + i
        copy = pltpu.make_async_remote_copy(
            src_ref=f_send.at[layer, slot], dst_ref=f_recv.at[places[x]], send_sem=f_ssem.at[layer, slot],
            recv_sem=f_rsem.at[places[x]], device_id=target, device_id_type=MESH)
        return copy, jnp.logical_or(target[0] != p, target[1] != q)

    def to_holders(layer):
        width = SIDE * 128
        half = gd.rows_pad // 2
        for x in range(gd.x_lo):
            arrive(ring_copies[layer][x])
            mine = y if x == 0 else z

            def one(i, _):
                total = r_send[layer, x, mine, i].astype(F32)
                for d in range(1, gd.ring):
                    total = total + r_recv[layer, x, d, i].astype(F32)
                line[i] = total
                return 0

            lax.fori_loop(0, SIDE // 2, one, 0)
            whole = jnp.concatenate(
                [line[i, h * gd.columns:(h + 1) * gd.columns] for h in range(2) for i in range(SIDE // 2)], axis=1)
            shift = gd.rows * gd.quarter - (KERNEL - SIDE) * 128
            whole = jnp.where(core == 0, whole, pltpu.roll(whole, (width - shift) % width, 1))
            for i in range(gd.quarter):
                begin = i * gd.rows
                part = whole if begin == 0 else pltpu.roll(whole, width - begin, 1)
                chunk = jnp.concatenate([part[:, :half], part[:, half:gd.rows_pad]], axis=0)
                f_send[layer, x * gd.quarter + i] = chunk.astype(BF16)
            for i in range(gd.quarter):
                copy, away = f_copy(layer, x, i)

                @pl.when(away)
                def _():
                    copy.start()

                @pl.when(jnp.logical_not(away))
                def _():
                    f_recv[places[x]] = f_send[layer, x * gd.quarter + i]

    pl.semaphore_wait(barrier, greeted)
    start(act_copies)
    got_cot.wait()
    got_w2.wait()
    got_inv.wait()
    halo_partial(g_ext, w2, 1)
    start(back_copies[1])
    start(feat_copies)
    turn(g_ext)
    own_partial(g_ext, w2)
    got_in_tab.wait()
    got_out_tab.wait()
    arrive_halo(act_copies, act_ext, BLOCKS, -1)
    weight_terms(act_ext, 1)
    to_rings(1)
    arrive_halo(back_copies[1], rb_g2, 0, 1)

    def slope(b, _):
        value = pre[b].astype(F32)
        gate = sigmoid(value)
        pg_ext[b] = (with_returned(b, 1) * (gate * (1.0 + value * (1.0 - gate)))).astype(BF16)
        return 0

    lax.fori_loop(0, BLOCKS, slope, 0)
    turn(pg_ext)
    got_feat_ext.wait()
    got_w1.wait()
    arrive_halo(feat_copies, feat_ext, BLOCKS, -1)
    weight_terms(feat_ext, 0)
    to_rings(0)
    halo_partial(pg_ext, w1, 0)
    start(back_copies[0])
    to_holders(1)
    own_partial(pg_ext, w1)
    to_holders(0)
    arrive_halo(back_copies[0], rb_g1, 0, 1)

    def finish(b, _):
        grad_out[b] = with_returned(b, 0).astype(BF16)
        return 0

    lax.fori_loop(0, BLOCKS, finish, 0)
    stored = load(12, grad_out, grad_hbm)

    own_place = jnp.where(xl == 0, places[0], places[1])
    holds_own = jnp.logical_and(sender_core == core, jnp.where(xl == 0, y, z) == z)

    def others(s, _):
        @pl.when(jnp.logical_not(jnp.logical_and(s == own_place, holds_own)))
        def _():
            pltpu.make_async_remote_copy(
                src_ref=f_send.at[0, 0], dst_ref=f_recv.at[s], send_sem=f_ssem.at[0, 0],
                recv_sem=f_rsem.at[s], device_id=(p, q + 1 - 2 * core), device_id_type=MESH).wait_recv()
        return 0

    lax.fori_loop(0, gd.sources, others, 0)
    total = f_recv[0].astype(F32)
    for s in range(1, gd.sources):
        total = total + f_recv[s].astype(F32)
    total = total * (1.0 / math.sqrt(MAP_CAP * BLOCK * gd.n_gx * gd.n_gy))
    total = jnp.concatenate([total[:gd.columns], total[gd.columns:]], axis=1)
    weight_out[...] = total[:, :gd.rows]

    for copies in [act_copies, feat_copies, core_copies] + back_copies + ring_copies[0] + ring_copies[1]:
        for copy in copies:
            copy.wait_send()
    for layer in range(2):
        for x in range(gd.x_lo):
            for i in range(gd.quarter):
                copy, away = f_copy(layer, x, i)

                @pl.when(away)
                def _():
                    copy.wait_send()
    stored.wait()


def per_device(grid, features_in, pre_act, cotangent, w_first, w_second, in_slots, out_slots, send_lists):
    gd = grid
    slots_in = jnp.transpose(in_slots[0], (2, 0, 1))
    slots_out = jnp.transpose(out_slots[0], (2, 0, 1))
    sends = jnp.transpose(send_lists[0, 0])
    ext = ZERO + 1
    half = gd.rows_pad // 2
    dma = pltpu.SemaphoreType.DMA
    block = (BLOCK, 128)
    slots = (MAP_CAP, 1, KERNEL)
    hbm = pl.BlockSpec(memory_space=pltpu.HBM)
    flops = 2 * 128 ** 3 * KERNEL * 2 * (ZERO + MAP_CAP)
    grad, weight = pl.pallas_call(
        functools.partial(kernel, gd),
        out_shape=(
            jax.ShapeDtypeStruct((BLOCKS,) + block, BF16),
            jax.ShapeDtypeStruct((gd.columns, gd.rows), F32),
        ),
        in_specs=[hbm] * 8,
        out_specs=(hbm, pl.BlockSpec(memory_space=pltpu.VMEM)),
        scratch_shapes=[
            pltpu.VMEM(slots, jnp.int32),
            pltpu.VMEM(slots, jnp.int32),
            pltpu.VMEM((32, 128), jnp.int32),
            pltpu.SMEM(slots, jnp.int32),
            pltpu.SMEM(slots, jnp.int32),
            pltpu.SMEM((SEND_CAP, 8), jnp.int32),
            pltpu.SMEM((32, 128), jnp.int32),
            pltpu.VMEM((BLOCKS,) + block, BF16),
            pltpu.VMEM((BLOCKS,) + block, BF16),
            pltpu.VMEM((KERNEL,) + block, BF16),
            pltpu.VMEM((KERNEL,) + block, BF16),
            pltpu.VMEM((BLOCKS,) + block, BF16),
            pltpu.VMEM((BLOCKS,) + block, BF16),
            pltpu.VMEM((ext,) + block, BF16),
            pltpu.VMEM((ext,) + block, BF16),
            pltpu.VMEM((BLOCKS + 1,) + block, BF16),
            pltpu.VMEM((BLOCKS + 1,) + block, BF16),
            pltpu.VMEM((BLOCKS + 1,) + block, BF16),
            pltpu.VMEM((BLOCKS,) + block, F32),
            pltpu.VMEM((HALO,) + block, BF16),
            pltpu.VMEM((HALO,) + block, BF16),
            pltpu.VMEM((2, HALO) + block, BF16),
            pltpu.VMEM((HALO + 1,) + block, BF16),
            pltpu.VMEM((HALO + 1,) + block, BF16),
            pltpu.VMEM((2, SIDE) + block, BF16),
            pltpu.VMEM((2, SIDE) + block, BF16),
            pltpu.VMEM((SIDE,) + block, F32),
            pltpu.VMEM((2, gd.x_lo, gd.ring, SIDE // 2, 2 * gd.columns, 128), BF16),
            pltpu.VMEM((2, gd.x_lo, gd.ring, SIDE // 2, 2 * gd.columns, 128), BF16),
            pltpu.VMEM((SIDE // 2, 2 * gd.columns, 128), F32),
            pltpu.VMEM((2, gd.x_lo * gd.quarter, 2 * gd.columns, half), BF16),
            pltpu.VMEM((gd.sources, 2 * gd.columns, half), BF16),
            dma((13,)),
            dma((4, 8)),
            dma((4, 8)),
            dma((2,)),
            dma((2,)),
            dma((2, gd.x_lo, gd.ring)),
            dma((2, gd.x_lo, gd.ring)),
            dma((2, gd.x_lo * gd.quarter)),
            dma((gd.sources,)),
        ],
        compiler_params=pltpu.CompilerParams(
            collective_id=0, has_side_effects=True, vmem_limit_bytes=56 * 1024 * 1024
        ),
        cost_estimate=pl.CostEstimate(flops=flops, bytes_accessed=8 * 2 ** 20, transcendentals=0),
    )(slots_in, slots_out, sends, features_in[0, 0], pre_act[0, 0], cotangent[0, 0], w_first, w_second)
    return grad[None, None], weight.T


def build(mesh, x_lo, x_hi):
    grid = Grid(mesh.shape["gx"], mesh.shape["gy"], x_lo, x_hi)
    in_specs = (
        P("gx", "gy", None, None, None),
        P("gx", "gy", None, None, None),
        P("gx", "gy", None, None, None),
        P(),
        P(),
        P("gx", "gy", None, None),
        P("gx", "gy", None, None),
        P("gx", "gy", None, None),
    )
    out_specs = (P("gx", "gy", None, None, None), P("gy", "gx"))
    return jax.shard_map(
        functools.partial(per_device, grid), mesh=mesh, in_specs=in_specs, out_specs=out_specs, check_vma=False
    )


def solution(mesh):
    return build(mesh, 2, 2)
```

```python
import functools
import math

import jax
import jax.numpy as jnp
from jax import lax
from jax.experimental import pallas as pl
from jax.experimental.pallas import tpu as pltpu
from jax.sharding import PartitionSpec as P

HEADINGS = ((-1, -1), (-1, 0), (-1, 1), (0, -1), (0, 1), (1, -1), (1, 0), (1, 1))
KERNEL, MAP_CAP, BLOCKS, SEND_CAP, BLOCK = 27, 7, 12, 2, 128
HALO = 8 * SEND_CAP
ZERO = BLOCKS + HALO
SIDE = 14
ORDER = (5, 7, 0, 2, 3, 4, 6, 1)
MESH = pl.DeviceIdType.MESH
F32, BF16 = jnp.float32, jnp.bfloat16

class Grid:
    def __init__(self, n_gx, n_gy, x_lo, x_hi):
        self.n_gx, self.n_gy, self.x_lo, self.x_hi = n_gx, n_gy, x_lo, x_hi
        self.z = n_gx // x_lo
        self.y = n_gy // (2 * x_hi)
        self.chips = n_gy // 2
        self.columns = 128 // n_gx
        self.rows = 2 * KERNEL * 128 // n_gy
        self.rows_pad = -(-self.rows // 256) * 256
        self.half = n_gy // 2
        self.quarter = n_gy // 4
        self.ring = self.z
        self.sources = x_lo * x_hi * self.ring


def sigmoid(value):
    return 1.0 / (1.0 + jnp.exp(-value))


def kernel(grid, in_hbm, out_hbm, send_hbm, feat_hbm, pre_hbm, cot_hbm, w1_hbm, w2_hbm, grad_hbm, weight_out,
           in_vec, out_vec, inv_vec, in_tab, out_tab, send_tab, inv_tab, feat, pre, w1, w2, grad_out,
           act_own, act_ext, feat_ext, g_ext, pg_ext, gt, acc, sb_act, sb_feat, sb_g, rb_g1, rb_g2,
           core_send, core_recv, own, r_send, r_recv, line, f_send, f_recv,
           load_sem, halo_ssem, halo_rsem, core_ssem, core_rsem, r_ssem, r_rsem, f_ssem, f_rsem):
    gd = grid
    p, q = lax.axis_index("gx"), lax.axis_index("gy")
    z, xl = p % gd.z, p // gd.z
    core, chip_q = q % 2, q // 2
    y, xh = chip_q // gd.x_hi, chip_q % gd.x_hi

    def load(n, src, dst):
        copy = pltpu.make_async_copy(src, dst, load_sem.at[n])
        copy.start()
        return copy

    got_in = load(0, in_hbm, in_vec)
    got_out = load(1, out_hbm, out_vec)
    got_send = load(2, send_hbm, send_tab)
    got_pre = load(3, pre_hbm, pre)
    got_feat = load(4, feat_hbm, feat)
    got_cot = load(5, cot_hbm, g_ext.at[pl.ds(0, BLOCKS)])
    got_w2 = load(6, w2_hbm, w2)
    got_in_tab = load(7, in_hbm, in_tab)
    got_out_tab = load(8, out_hbm, out_tab)
    got_feat_ext = load(9, feat_hbm, feat_ext.at[pl.ds(0, BLOCKS)])
    got_w1 = load(10, w1_hbm, w1)

    barrier = pltpu.get_barrier_semaphore()

    def hello(px, qy):
        pl.semaphore_signal(barrier, inc=1, device_id=(px, qy), device_id_type=MESH)

    sender_core = (q % gd.half) // gd.quarter

    def hello_source(s, _):
        x, i = s // gd.ring, s % gd.ring
        px = jnp.where(xl == 0, (x // gd.x_hi) * gd.z + i, (x // gd.x_hi) * gd.z + z)
        qy = (jnp.where(xl == 0, z, i) * gd.x_hi + x % gd.x_hi) * 2 + sender_core
        hello(px, qy)
        return 0

    lax.fori_loop(0, gd.sources, hello_source, 0)
    for d in range(1, gd.ring):
        hello(xl * gd.z + (z + d) % gd.z, q)
        hello(p, (((y + d) % gd.y) * gd.x_hi + xh) * 2 + core)
    hello(p, q + 1 - 2 * core)
    for a, b in HEADINGS:
        hello((p + a + gd.n_gx) % gd.n_gx, (q + b + gd.n_gy) % gd.n_gy)
    greeted = 2 * gd.x_lo * gd.quarter + 2 * (gd.ring - 1) + 1 + 8

    zero_block = jnp.zeros((BLOCK, 128), BF16)
    returned = (rb_g1, rb_g2)
    for buffer, place in ((act_ext, ZERO), (feat_ext, ZERO), (g_ext, BLOCKS), (pg_ext, BLOCKS), (gt, BLOCKS),
                          (rb_g1, HALO), (rb_g2, HALO)):
        buffer[place] = zero_block

    got_in.wait()
    got_out.wait()
    inv_vec[...] = jnp.zeros(inv_vec.shape, jnp.int32)
    slots = lax.broadcasted_iota(jnp.int32, (ZERO, KERNEL), 0)
    inverse = jnp.full((ZERO, KERNEL), BLOCKS, jnp.int32)
    for m in range(MAP_CAP):
        inverse = jnp.where(in_vec[m] == slots, out_vec[m], inverse)
    inv_vec[:ZERO, :KERNEL] = inverse
    got_inv = load(11, inv_vec, inv_tab)

    got_pre.wait()

    def load_own(b, _):
        value = pre[b].astype(F32)
        value = (value * sigmoid(value)).astype(BF16)
        act_own[b] = value
        act_ext[b] = value
        return 0

    lax.fori_loop(0, BLOCKS, load_own, 0)
    got_send.wait()
    got_feat.wait()

    def pick(e, _):
        for s in range(SEND_CAP):
            sb_act[2 * e + s] = act_own[send_tab[s, e]]
            sb_feat[2 * e + s] = feat[send_tab[s, e]]
        return 0

    lax.fori_loop(0, 8, pick, 0)

    def halo_copy(kind, e, src, dst, a, b):
        return pltpu.make_async_remote_copy(
            src_ref=src, dst_ref=dst, send_sem=halo_ssem.at[kind, e], recv_sem=halo_rsem.at[kind, e],
            device_id=((p + a + gd.n_gx) % gd.n_gx, (q + b + gd.n_gy) % gd.n_gy), device_id_type=MESH)

    def forth(kind, src, ext):
        return [halo_copy(kind, e, src.at[pl.ds(2 * e, 2)], ext.at[pl.ds(BLOCKS + 2 * e, 2)], a, b)
                for e, (a, b) in enumerate(HEADINGS)]

    def back(kind, layer):
        return [halo_copy(kind, e, sb_g.at[layer, pl.ds(2 * e, 2)], returned[layer].at[pl.ds(2 * e, 2)], -a, -b)
                for e, (a, b) in enumerate(HEADINGS)]

    def start(copies):
        for copy in copies:
            copy.start()

    def arrive(copies):
        for copy in copies:
            copy.wait_recv()

    def inside(a, b):
        px, qy = p + a, q + b
        return (px >= 0) & (px < gd.n_gx) & (qy >= 0) & (qy < gd.n_gy)

    def each_inside(copies, sign, act):
        for e in ORDER:
            a, b = HEADINGS[e]

            @pl.when(inside(sign * a, sign * b))
            def _():
                act(copies[e])

    def start_halo(copies, sign):
        each_inside(copies, sign, lambda copy: copy.start())

    def arrive_halo(copies, buffer, first, sign):
        each_inside(copies, -sign, lambda copy: copy.wait_recv())
        for e, (a, b) in enumerate(HEADINGS):
            @pl.when(jnp.logical_not(inside(-sign * a, -sign * b)))
            def _():
                for s in range(SEND_CAP):
                    buffer[first + 2 * e + s] = zero_block

    act_copies, feat_copies = forth(0, sb_act, act_ext), forth(1, sb_feat, feat_ext)
    back_copies = [back(3, 0), back(2, 1)]

    def products(grads, weight, j, n):
        lhs = jnp.concatenate(
            [jnp.concatenate([grads[inv_tab[j + t, k]] for k in range(KERNEL)], axis=1) for t in range(n)], axis=0)
        rhs = jnp.concatenate([weight[k] for k in range(KERNEL)], axis=1)
        out = lax.dot_general(lhs, rhs, (((1,), (1,)), ((), ())), preferred_element_type=F32)
        return out.reshape(n, BLOCK, 128)

    def halo_partial(grads, weight, layer):
        def group(i, _):
            sb_g[layer, pl.ds(4 * i, 4)] = products(grads, weight, BLOCKS + 4 * i, 4).astype(BF16)
            return 0

        lax.fori_loop(0, HALO // 4, group, 0)

    def own_partial(grads, weight, groups=(0, BLOCKS // 4)):
        def group(i, _):
            acc[pl.ds(4 * i, 4)] = products(grads, weight, 4 * i, 4)
            return 0

        lax.fori_loop(*groups, group, 0)

    def with_returned(b, layer):
        total = acc[b]
        for e in range(8):
            place = jnp.where(send_tab[0, e] == b, 2 * e, jnp.where(send_tab[1, e] == b, 2 * e + 1, HALO))
            total = total + returned[layer][place].astype(F32)
        return total

    def turn(grads):
        def one(b, _):
            gt[b] = grads[b].T
            return 0

        lax.fori_loop(0, BLOCKS, one, 0)

    def weight_term(sources, k):
        lhs = jnp.concatenate([gt[out_tab[m, 0, k]] for m in range(MAP_CAP)], axis=1)
        rhs = jnp.concatenate([sources[in_tab[m, 0, k]] for m in range(MAP_CAP)], axis=0)
        return lax.dot_general(lhs, rhs, (((1,), (0,)), ((), ())), preferred_element_type=F32)

    def core_copy(layer):
        return pltpu.make_async_remote_copy(
            src_ref=core_send.at[layer], dst_ref=core_recv.at[layer], send_sem=core_ssem.at[layer],
            recv_sem=core_rsem.at[layer], device_id=(p, q + 1 - 2 * core), device_id_type=MESH)

    first_k = core * (KERNEL - SIDE)
    other_k = (1 - core) * (KERNEL - SIDE)
    core_copies = [core_copy(0), core_copy(1)]

    def weight_terms(sources, layer):
        def other(i, _):
            for u in range(7):
                core_send[layer, 7 * i + u] = weight_term(sources, other_k + 7 * i + u).astype(BF16)
            return 0

        lax.fori_loop(0, SIDE // 7, other, 0)
        core_copies[layer].start()

        def mine(i, _):
            for u in range(7):
                own[7 * i + u] = weight_term(sources, first_k + 7 * i + u)
            return 0

        lax.fori_loop(0, SIDE // 7, mine, 0)

    def ring_copy(layer, x, d):
        if x == 0:
            there = (y + d) % gd.y
            target = (p, (there * gd.x_hi + xh) * 2 + core)
        else:
            there = (z + d) % gd.z
            target = (xl * gd.z + there, q)
        return pltpu.make_async_remote_copy(
            src_ref=r_send.at[layer, x, there], dst_ref=r_recv.at[layer, x, d], send_sem=r_ssem.at[layer, x, d],
            recv_sem=r_rsem.at[layer, x, d], device_id=target, device_id_type=MESH)

    ring_copies = [[[ring_copy(layer, x, d) for d in range(1, gd.ring)] for x in range(gd.x_lo)] for layer in range(2)]

    def to_rings(layer):
        core_copies[layer].wait_recv()

        def one(i, _):
            low = own[i] + core_recv[layer, i].astype(F32)
            high = own[i + SIDE // 2] + core_recv[layer, i + SIDE // 2].astype(F32)
            for x in range(gd.x_lo):
                for c in range(gd.ring):
                    rows = slice((x * gd.ring + c) * gd.columns, (x * gd.ring + c + 1) * gd.columns)
                    r_send[layer, x, c, i] = jnp.concatenate([low[rows], high[rows]], axis=0).astype(BF16)
            return 0

        lax.fori_loop(0, SIDE // 2, one, 0)
        for x in range(gd.x_lo):
            start(ring_copies[layer][x])

    places = [(xl * gd.x_hi + xh) * gd.ring + z, (xl * gd.x_hi + xh) * gd.ring + y]

    def f_copy(layer, x, i):
        column = y if x == 0 else z
        target = (x * gd.z + column, layer * gd.half + core * gd.quarter + i)
        slot = x * gd.quarter + i
        copy = pltpu.make_async_remote_copy(
            src_ref=f_send.at[layer, slot], dst_ref=f_recv.at[places[x]], send_sem=f_ssem.at[layer, slot],
            recv_sem=f_rsem.at[places[x]], device_id=target, device_id_type=MESH)
        return copy, jnp.logical_or(target[0] != p, target[1] != q)

    def to_holders(layer):
        width = SIDE * 128
        half = gd.rows_pad // 2
        for x in range(gd.x_lo):
            arrive(ring_copies[layer][x])
            mine = y if x == 0 else z

            def one(i, _):
                total = r_send[layer, x, mine, i].astype(F32)
                for d in range(1, gd.ring):
                    total = total + r_recv[layer, x, d, i].astype(F32)
                line[i] = total
                return 0

            lax.fori_loop(0, SIDE // 2, one, 0)
            whole = jnp.concatenate(
                [line[i, h * gd.columns:(h + 1) * gd.columns] for h in range(2) for i in range(SIDE // 2)], axis=1)
            shift = gd.rows * gd.quarter - (KERNEL - SIDE) * 128
            whole = jnp.where(core == 0, whole, pltpu.roll(whole, (width - shift) % width, 1))
            for i in range(gd.quarter):
                begin = i * gd.rows
                part = whole if begin == 0 else pltpu.roll(whole, width - begin, 1)
                chunk = jnp.concatenate([part[:, :half], part[:, half:gd.rows_pad]], axis=0)
                f_send[layer, x * gd.quarter + i] = chunk.astype(BF16)
            for i in range(gd.quarter):
                copy, away = f_copy(layer, x, i)

                @pl.when(away)
                def _():
                    copy.start()

                @pl.when(jnp.logical_not(away))
                def _():
                    f_recv[places[x]] = f_send[layer, x * gd.quarter + i]

    pl.semaphore_wait(barrier, greeted)
    start_halo(act_copies, 1)
    got_cot.wait()
    got_w2.wait()
    got_inv.wait()
    halo_partial(g_ext, w2, 1)
    start_halo(back_copies[1], -1)
    turn(g_ext)
    own_partial(g_ext, w2, (0, 1))
    start_halo(feat_copies, 1)
    own_partial(g_ext, w2, (1, BLOCKS // 4))
    got_in_tab.wait()
    got_out_tab.wait()
    arrive_halo(act_copies, act_ext, BLOCKS, 1)
    weight_terms(act_ext, 1)
    to_rings(1)
    arrive_halo(back_copies[1], rb_g2, 0, -1)

    def slope(b, _):
        value = pre[b].astype(F32)
        gate = sigmoid(value)
        pg_ext[b] = (with_returned(b, 1) * (gate * (1.0 + value * (1.0 - gate)))).astype(BF16)
        return 0

    lax.fori_loop(0, BLOCKS, slope, 0)
    turn(pg_ext)
    got_feat_ext.wait()
    got_w1.wait()
    arrive_halo(feat_copies, feat_ext, BLOCKS, 1)
    weight_terms(feat_ext, 0)
    to_rings(0)
    halo_partial(pg_ext, w1, 0)
    start_halo(back_copies[0], -1)
    to_holders(1)
    own_partial(pg_ext, w1)
    to_holders(0)
    arrive_halo(back_copies[0], rb_g1, 0, -1)

    def finish(b, _):
        grad_out[b] = with_returned(b, 0)
        return 0

    lax.fori_loop(0, BLOCKS, finish, 0)

    stored = load(12, grad_out, grad_hbm)

    own_place = jnp.where(xl == 0, places[0], places[1])
    holds_own = jnp.logical_and(sender_core == core, jnp.where(xl == 0, y, z) == z)

    def others(s, _):
        @pl.when(jnp.logical_not(jnp.logical_and(s == own_place, holds_own)))
        def _():
            pltpu.make_async_remote_copy(
                src_ref=f_send.at[0, 0], dst_ref=f_recv.at[s], send_sem=f_ssem.at[0, 0],
                recv_sem=f_rsem.at[s], device_id=(p, q + 1 - 2 * core), device_id_type=MESH).wait_recv()
        return 0

    lax.fori_loop(0, gd.sources, others, 0)
    total = f_recv[0].astype(F32)
    for s in range(1, gd.sources):
        total = total + f_recv[s].astype(F32)
    total = jnp.concatenate([total[:gd.columns], total[gd.columns:]], axis=1)
    weight_out[...] = total[:, :gd.rows]

    for copies, sign in ((act_copies, 1), (feat_copies, 1), (back_copies[0], -1), (back_copies[1], -1)):
        each_inside(copies, sign, lambda copy: copy.wait_send())
    for copies in [core_copies] + ring_copies[0] + ring_copies[1]:
        for copy in copies:
            copy.wait_send()
    for layer in range(2):
        for x in range(gd.x_lo):
            for i in range(gd.quarter):
                copy, away = f_copy(layer, x, i)

                @pl.when(away)
                def _():
                    copy.wait_send()
    stored.wait()


def per_device(grid, features_in, pre_act, cotangent, w_first, w_second, in_slots, out_slots, send_lists):
    gd = grid
    slots_in = jnp.transpose(in_slots[0], (2, 0, 1))
    slots_out = jnp.transpose(out_slots[0], (2, 0, 1))
    sends = jnp.transpose(send_lists[0, 0])
    ext = ZERO + 1
    half = gd.rows_pad // 2
    dma = pltpu.SemaphoreType.DMA
    block = (BLOCK, 128)
    slots = (MAP_CAP, 1, KERNEL)
    hbm, vmem = pl.BlockSpec(memory_space=pltpu.HBM), pl.BlockSpec(memory_space=pltpu.VMEM)
    flops = 2 * 128 ** 3 * KERNEL * 2 * (ZERO + MAP_CAP)
    grad, weight = pl.pallas_call(
        functools.partial(kernel, gd),
        out_shape=(
            jax.ShapeDtypeStruct((BLOCKS,) + block, F32),
            jax.ShapeDtypeStruct((gd.columns, gd.rows), F32),
        ),
        in_specs=[hbm] * 8,
        out_specs=(hbm, vmem),
        scratch_shapes=[
            pltpu.VMEM(slots, jnp.int32),
            pltpu.VMEM(slots, jnp.int32),
            pltpu.VMEM((32, 128), jnp.int32),
            pltpu.SMEM(slots, jnp.int32),
            pltpu.SMEM(slots, jnp.int32),
            pltpu.SMEM((SEND_CAP, 8), jnp.int32),
            pltpu.SMEM((32, 128), jnp.int32),
            pltpu.VMEM((BLOCKS,) + block, BF16),
            pltpu.VMEM((BLOCKS,) + block, BF16),
            pltpu.VMEM((KERNEL,) + block, BF16),
            pltpu.VMEM((KERNEL,) + block, BF16),
            pltpu.VMEM((BLOCKS,) + block, F32),
            pltpu.VMEM((BLOCKS,) + block, BF16),
            pltpu.VMEM((ext,) + block, BF16),
            pltpu.VMEM((ext,) + block, BF16),
            pltpu.VMEM((BLOCKS + 1,) + block, BF16),
            pltpu.VMEM((BLOCKS + 1,) + block, BF16),
            pltpu.VMEM((BLOCKS + 1,) + block, BF16),
            pltpu.VMEM((BLOCKS,) + block, F32),
            pltpu.VMEM((HALO,) + block, BF16),
            pltpu.VMEM((HALO,) + block, BF16),
            pltpu.VMEM((2, HALO) + block, BF16),
            pltpu.VMEM((HALO + 1,) + block, BF16),
            pltpu.VMEM((HALO + 1,) + block, BF16),
            pltpu.VMEM((2, SIDE) + block, BF16),
            pltpu.VMEM((2, SIDE) + block, BF16),
            pltpu.VMEM((SIDE,) + block, F32),
            pltpu.VMEM((2, gd.x_lo, gd.ring, SIDE // 2, 2 * gd.columns, 128), BF16),
            pltpu.VMEM((2, gd.x_lo, gd.ring, SIDE // 2, 2 * gd.columns, 128), BF16),
            pltpu.VMEM((SIDE // 2, 2 * gd.columns, 128), F32),
            pltpu.VMEM((2, gd.x_lo * gd.quarter, 2 * gd.columns, half), BF16),
            pltpu.VMEM((gd.sources, 2 * gd.columns, half), BF16),
            dma((13,)),
            dma((4, 8)),
            dma((4, 8)),
            dma((2,)),
            dma((2,)),
            dma((2, gd.x_lo, gd.ring)),
            dma((2, gd.x_lo, gd.ring)),
            dma((2, gd.x_lo * gd.quarter)),
            dma((gd.sources,)),
        ],
        compiler_params=pltpu.CompilerParams(
            collective_id=0, has_side_effects=True, vmem_limit_bytes=56 * 1024 * 1024
        ),
        cost_estimate=pl.CostEstimate(flops=flops, bytes_accessed=8 * 2 ** 20, transcendentals=0),
    )(slots_in, slots_out, sends, features_in[0, 0], pre_act[0, 0], cotangent[0, 0], w_first, w_second)
    weight = weight.T * (1.0 / math.sqrt(MAP_CAP * BLOCK * gd.n_gx * gd.n_gy))
    return grad.astype(BF16)[None, None], weight


def build(mesh, x_lo, x_hi):
    grid = Grid(mesh.shape["gx"], mesh.shape["gy"], x_lo, x_hi)
    in_specs = (
        P("gx", "gy", None, None, None),
        P("gx", "gy", None, None, None),
        P("gx", "gy", None, None, None),
        P(),
        P(),
        P("gx", "gy", None, None),
        P("gx", "gy", None, None),
        P("gx", "gy", None, None),
    )
    out_specs = (P("gx", "gy", None, None, None), P("gy", "gx"))
    return jax.shard_map(
        functools.partial(per_device, grid), mesh=mesh, in_specs=in_specs, out_specs=out_specs, check_vma=False
    )


def solution(mesh):
    return build(mesh, 2, 2)
```

```python
import functools
import math

import jax
import jax.numpy as jnp
from jax import lax
from jax.experimental import pallas as pl
from jax.experimental.pallas import tpu as pltpu
from jax.sharding import PartitionSpec as P

HEADINGS = ((-1, -1), (-1, 0), (-1, 1), (0, -1), (0, 1), (1, -1), (1, 0), (1, 1))
KERNEL, MAP_CAP, BLOCKS, SEND_CAP, BLOCK = 27, 7, 12, 2, 128
HALO = 8 * SEND_CAP
ZERO = BLOCKS + HALO
SIDE = 14
ORDER = (5, 7, 0, 2, 3, 4, 6, 1)
MESH = pl.DeviceIdType.MESH
F32, BF16 = jnp.float32, jnp.bfloat16

class Grid:
    def __init__(self, n_gx, n_gy, x_lo, x_hi):
        self.n_gx, self.n_gy, self.x_lo, self.x_hi = n_gx, n_gy, x_lo, x_hi
        self.z = n_gx // x_lo
        self.y = n_gy // (2 * x_hi)
        self.chips = n_gy // 2
        self.columns = 128 // n_gx
        self.rows = 2 * KERNEL * 128 // n_gy
        self.rows_pad = -(-self.rows // 256) * 256
        self.half = n_gy // 2
        self.quarter = n_gy // 4
        self.ring = self.z
        self.sources = x_lo * x_hi * self.ring


def sigmoid(value):
    return 1.0 / (1.0 + jnp.exp(-value))


def kernel(grid, in_hbm, out_hbm, send_hbm, feat_hbm, pre_hbm, cot_hbm, w1_hbm, w2_hbm, grad_hbm, weight_out,
           in_vec, out_vec, inv_vec, in_tab, out_tab, send_tab, inv_tab, feat, pre, w1, w2, grad_out,
           act_own, act_ext, feat_ext, g_ext, pg_ext, gt, acc, sb_act, sb_feat, sb_g, rb_g1, rb_g2,
           core_send, core_recv, own, r_send, r_recv, line, f_send, f_recv,
           load_sem, halo_ssem, halo_rsem, core_ssem, core_rsem, r_ssem, r_rsem, f_ssem, f_rsem):
    gd = grid
    p, q = lax.axis_index("gx"), lax.axis_index("gy")
    z, xl = p % gd.z, p // gd.z
    core, chip_q = q % 2, q // 2
    y, xh = chip_q // gd.x_hi, chip_q % gd.x_hi

    def load(n, src, dst):
        copy = pltpu.make_async_copy(src, dst, load_sem.at[n])
        copy.start()
        return copy

    got_in = load(0, in_hbm, in_vec)
    got_out = load(1, out_hbm, out_vec)
    got_send = load(2, send_hbm, send_tab)
    got_pre = load(3, pre_hbm, pre)
    got_feat = load(4, feat_hbm, feat)
    got_cot = load(5, cot_hbm, g_ext.at[pl.ds(0, BLOCKS)])
    got_w2 = load(6, w2_hbm, w2)
    got_in_tab = load(7, in_hbm, in_tab)
    got_out_tab = load(8, out_hbm, out_tab)
    got_feat_ext = load(9, feat_hbm, feat_ext.at[pl.ds(0, BLOCKS)])
    got_w1 = load(10, w1_hbm, w1)

    barrier = pltpu.get_barrier_semaphore()

    def hello(px, qy):
        pl.semaphore_signal(barrier, inc=1, device_id=(px, qy), device_id_type=MESH)

    sender_core = (q % gd.half) // gd.quarter

    def hello_source(s, _):
        x, i = s // gd.ring, s % gd.ring
        px = jnp.where(xl == 0, (x // gd.x_hi) * gd.z + i, (x // gd.x_hi) * gd.z + z)
        qy = (jnp.where(xl == 0, z, i) * gd.x_hi + x % gd.x_hi) * 2 + sender_core
        hello(px, qy)
        return 0

    lax.fori_loop(0, gd.sources, hello_source, 0)
    for d in range(1, gd.ring):
        hello(xl * gd.z + (z + d) % gd.z, q)
        hello(p, (((y + d) % gd.y) * gd.x_hi + xh) * 2 + core)
    hello(p, q + 1 - 2 * core)
    for a, b in HEADINGS:
        hello((p + a + gd.n_gx) % gd.n_gx, (q + b + gd.n_gy) % gd.n_gy)
    greeted = 2 * gd.x_lo * gd.quarter + 2 * (gd.ring - 1) + 1 + 8

    zero_block = jnp.zeros((BLOCK, 128), BF16)
    returned = (rb_g1, rb_g2)
    for buffer, place in ((act_ext, ZERO), (feat_ext, ZERO), (g_ext, BLOCKS), (pg_ext, BLOCKS), (gt, BLOCKS),
                          (rb_g1, HALO), (rb_g2, HALO)):
        buffer[place] = zero_block

    got_in.wait()
    got_out.wait()
    inv_vec[...] = jnp.zeros(inv_vec.shape, jnp.int32)
    slots = lax.broadcasted_iota(jnp.int32, (ZERO, KERNEL), 0)
    inverse = jnp.full((ZERO, KERNEL), BLOCKS, jnp.int32)
    for m in range(MAP_CAP):
        inverse = jnp.where(in_vec[m] == slots, out_vec[m], inverse)
    inv_vec[:ZERO, :KERNEL] = inverse
    got_inv = load(11, inv_vec, inv_tab)

    got_pre.wait()

    def load_own(b, _):
        value = pre[b].astype(F32)
        value = (value * sigmoid(value)).astype(BF16)
        act_own[b] = value
        act_ext[b] = value
        return 0

    lax.fori_loop(0, BLOCKS, load_own, 0)
    got_send.wait()
    got_feat.wait()

    def pick(e, _):
        for s in range(SEND_CAP):
            sb_act[2 * e + s] = act_own[send_tab[s, e]]
            sb_feat[2 * e + s] = feat[send_tab[s, e]]
        return 0

    lax.fori_loop(0, 8, pick, 0)

    def halo_copy(kind, e, src, dst, a, b):
        return pltpu.make_async_remote_copy(
            src_ref=src, dst_ref=dst, send_sem=halo_ssem.at[kind, e], recv_sem=halo_rsem.at[kind, e],
            device_id=((p + a + gd.n_gx) % gd.n_gx, (q + b + gd.n_gy) % gd.n_gy), device_id_type=MESH)

    def forth(kind, src, ext):
        return [halo_copy(kind, e, src.at[pl.ds(2 * e, 2)], ext.at[pl.ds(BLOCKS + 2 * e, 2)], a, b)
                for e, (a, b) in enumerate(HEADINGS)]

    def back(kind, layer):
        return [halo_copy(kind, e, sb_g.at[layer, pl.ds(2 * e, 2)], returned[layer].at[pl.ds(2 * e, 2)], -a, -b)
                for e, (a, b) in enumerate(HEADINGS)]

    def start(copies):
        for copy in copies:
            copy.start()

    def arrive(copies):
        for copy in copies:
            copy.wait_recv()

    def inside(a, b):
        px, qy = p + a, q + b
        return (px >= 0) & (px < gd.n_gx) & (qy >= 0) & (qy < gd.n_gy)

    def each_inside(copies, sign, act):
        for e in ORDER:
            e = e if sign > 0 else 7 - e
            a, b = HEADINGS[e]

            @pl.when(inside(sign * a, sign * b))
            def _():
                act(copies[e])

    def start_halo(copies, sign):
        each_inside(copies, sign, lambda copy: copy.start())

    def arrive_halo(copies, buffer, first, sign):
        each_inside(copies, -sign, lambda copy: copy.wait_recv())
        for e, (a, b) in enumerate(HEADINGS):
            @pl.when(jnp.logical_not(inside(-sign * a, -sign * b)))
            def _():
                for s in range(SEND_CAP):
                    buffer[first + 2 * e + s] = zero_block

    act_copies, feat_copies = forth(0, sb_act, act_ext), forth(1, sb_feat, feat_ext)
    back_copies = [back(3, 0), back(2, 1)]

    def products(grads, weight, j, n):
        lhs = jnp.concatenate(
            [jnp.concatenate([grads[inv_tab[j + t, k]] for k in range(KERNEL)], axis=1) for t in range(n)], axis=0)
        rhs = jnp.concatenate([weight[k] for k in range(KERNEL)], axis=1)
        out = lax.dot_general(lhs, rhs, (((1,), (1,)), ((), ())), preferred_element_type=F32)
        return out.reshape(n, BLOCK, 128)

    def halo_partial(grads, weight, layer):
        def group(i, _):
            sb_g[layer, pl.ds(4 * i, 4)] = products(grads, weight, BLOCKS + 4 * i, 4).astype(BF16)
            return 0

        lax.fori_loop(0, HALO // 4, group, 0)

    def own_partial(grads, weight, groups=(0, BLOCKS // 4)):
        def group(i, _):
            acc[pl.ds(4 * i, 4)] = products(grads, weight, 4 * i, 4)
            return 0

        lax.fori_loop(*groups, group, 0)

    def with_returned(b, layer):
        total = acc[b]
        for e in range(8):
            place = jnp.where(send_tab[0, e] == b, 2 * e, jnp.where(send_tab[1, e] == b, 2 * e + 1, HALO))
            total = total + returned[layer][place].astype(F32)
        return total

    def turn(grads):
        def one(b, _):
            gt[b] = grads[b].T
            return 0

        lax.fori_loop(0, BLOCKS, one, 0)

    def weight_term(sources, k):
        lhs = jnp.concatenate([gt[out_tab[m, 0, k]] for m in range(MAP_CAP)], axis=1)
        rhs = jnp.concatenate([sources[in_tab[m, 0, k]] for m in range(MAP_CAP)], axis=0)
        return lax.dot_general(lhs, rhs, (((1,), (0,)), ((), ())), preferred_element_type=F32)

    def core_copy(layer):
        return pltpu.make_async_remote_copy(
            src_ref=core_send.at[layer], dst_ref=core_recv.at[layer], send_sem=core_ssem.at[layer],
            recv_sem=core_rsem.at[layer], device_id=(p, q + 1 - 2 * core), device_id_type=MESH)

    first_k = core * (KERNEL - SIDE)
    other_k = (1 - core) * (KERNEL - SIDE)
    core_copies = [core_copy(0), core_copy(1)]

    def weight_terms(sources, layer):
        def other(i, _):
            for u in range(7):
                core_send[layer, 7 * i + u] = weight_term(sources, other_k + 7 * i + u).astype(BF16)
            return 0

        lax.fori_loop(0, SIDE // 7, other, 0)
        core_copies[layer].start()

        def mine(i, _):
            for u in range(7):
                own[7 * i + u] = weight_term(sources, first_k + 7 * i + u)
            return 0

        lax.fori_loop(0, SIDE // 7, mine, 0)

    def ring_copy(layer, x, d):
        if x == 0:
            there = (y + d) % gd.y
            target = (p, (there * gd.x_hi + xh) * 2 + core)
        else:
            there = (z + d) % gd.z
            target = (xl * gd.z + there, q)
        return pltpu.make_async_remote_copy(
            src_ref=r_send.at[layer, x, there], dst_ref=r_recv.at[layer, x, d], send_sem=r_ssem.at[layer, x, d],
            recv_sem=r_rsem.at[layer, x, d], device_id=target, device_id_type=MESH)

    ring_copies = [[[ring_copy(layer, x, d) for d in range(1, gd.ring)] for x in range(gd.x_lo)] for layer in range(2)]

    def to_rings(layer):
        core_copies[layer].wait_recv()

        def one(i, _):
            low = own[i] + core_recv[layer, i].astype(F32)
            high = own[i + SIDE // 2] + core_recv[layer, i + SIDE // 2].astype(F32)
            for x in range(gd.x_lo):
                for c in range(gd.ring):
                    rows = slice((x * gd.ring + c) * gd.columns, (x * gd.ring + c + 1) * gd.columns)
                    r_send[layer, x, c, i] = jnp.concatenate([low[rows], high[rows]], axis=0).astype(BF16)
            return 0

        lax.fori_loop(0, SIDE // 2, one, 0)
        for x in range(gd.x_lo):
            start(ring_copies[layer][x])

    places = [(xl * gd.x_hi + xh) * gd.ring + z, (xl * gd.x_hi + xh) * gd.ring + y]

    def f_copy(layer, x, i):
        column = y if x == 0 else z
        target = (x * gd.z + column, layer * gd.half + core * gd.quarter + i)
        slot = x * gd.quarter + i
        copy = pltpu.make_async_remote_copy(
            src_ref=f_send.at[layer, slot], dst_ref=f_recv.at[places[x]], send_sem=f_ssem.at[layer, slot],
            recv_sem=f_rsem.at[places[x]], device_id=target, device_id_type=MESH)
        return copy, jnp.logical_or(target[0] != p, target[1] != q)

    def to_holders(layer):
        width = SIDE * 128
        half = gd.rows_pad // 2
        for x in range(gd.x_lo):
            arrive(ring_copies[layer][x])
            mine = y if x == 0 else z

            def one(i, _):
                total = r_send[layer, x, mine, i].astype(F32)
                for d in range(1, gd.ring):
                    total = total + r_recv[layer, x, d, i].astype(F32)
                line[i] = total
                return 0

            lax.fori_loop(0, SIDE // 2, one, 0)
            whole = jnp.concatenate(
                [line[i, h * gd.columns:(h + 1) * gd.columns] for h in range(2) for i in range(SIDE // 2)], axis=1)
            shift = gd.rows * gd.quarter - (KERNEL - SIDE) * 128
            whole = jnp.where(core == 0, whole, pltpu.roll(whole, (width - shift) % width, 1))
            for i in range(gd.quarter):
                begin = i * gd.rows
                part = whole if begin == 0 else pltpu.roll(whole, width - begin, 1)
                chunk = jnp.concatenate([part[:, :half], part[:, half:gd.rows_pad]], axis=0)
                f_send[layer, x * gd.quarter + i] = chunk.astype(BF16)
            for i in range(gd.quarter):
                copy, away = f_copy(layer, x, i)

                @pl.when(away)
                def _():
                    copy.start()

                @pl.when(jnp.logical_not(away))
                def _():
                    f_recv[places[x]] = f_send[layer, x * gd.quarter + i]

    pl.semaphore_wait(barrier, greeted)
    start_halo(act_copies, 1)
    got_cot.wait()
    got_w2.wait()
    got_inv.wait()
    halo_partial(g_ext, w2, 1)
    start_halo(back_copies[1], -1)
    turn(g_ext)
    own_partial(g_ext, w2, (0, 1))
    start_halo(feat_copies, 1)
    own_partial(g_ext, w2, (1, BLOCKS // 4))
    got_in_tab.wait()
    got_out_tab.wait()
    arrive_halo(act_copies, act_ext, BLOCKS, 1)
    weight_terms(act_ext, 1)
    to_rings(1)
    arrive_halo(back_copies[1], rb_g2, 0, -1)

    def slope(b, _):
        value = pre[b].astype(F32)
        gate = sigmoid(value)
        pg_ext[b] = (with_returned(b, 1) * (gate * (1.0 + value * (1.0 - gate)))).astype(BF16)
        return 0

    lax.fori_loop(0, BLOCKS, slope, 0)
    turn(pg_ext)
    got_feat_ext.wait()
    got_w1.wait()
    arrive_halo(feat_copies, feat_ext, BLOCKS, 1)
    weight_terms(feat_ext, 0)
    to_rings(0)
    halo_partial(pg_ext, w1, 0)
    start_halo(back_copies[0], -1)
    to_holders(1)
    own_partial(pg_ext, w1)
    to_holders(0)
    arrive_halo(back_copies[0], rb_g1, 0, -1)

    def finish(b, _):
        grad_out[b] = with_returned(b, 0)
        return 0

    lax.fori_loop(0, BLOCKS, finish, 0)

    stored = load(12, grad_out, grad_hbm)

    own_place = jnp.where(xl == 0, places[0], places[1])
    holds_own = jnp.logical_and(sender_core == core, jnp.where(xl == 0, y, z) == z)

    def others(s, _):
        @pl.when(jnp.logical_not(jnp.logical_and(s == own_place, holds_own)))
        def _():
            pltpu.make_async_remote_copy(
                src_ref=f_send.at[0, 0], dst_ref=f_recv.at[s], send_sem=f_ssem.at[0, 0],
                recv_sem=f_rsem.at[s], device_id=(p, q + 1 - 2 * core), device_id_type=MESH).wait_recv()
        return 0

    lax.fori_loop(0, gd.sources, others, 0)
    total = f_recv[0].astype(F32)
    for s in range(1, gd.sources):
        total = total + f_recv[s].astype(F32)
    total = jnp.concatenate([total[:gd.columns], total[gd.columns:]], axis=1)
    weight_out[...] = total[:, :gd.rows]

    for copies, sign in ((act_copies, 1), (feat_copies, 1), (back_copies[0], -1), (back_copies[1], -1)):
        each_inside(copies, sign, lambda copy: copy.wait_send())
    for copies in [core_copies] + ring_copies[0] + ring_copies[1]:
        for copy in copies:
            copy.wait_send()
    for layer in range(2):
        for x in range(gd.x_lo):
            for i in range(gd.quarter):
                copy, away = f_copy(layer, x, i)

                @pl.when(away)
                def _():
                    copy.wait_send()
    stored.wait()


def per_device(grid, features_in, pre_act, cotangent, w_first, w_second, in_slots, out_slots, send_lists):
    gd = grid
    slots_in = jnp.transpose(in_slots[0], (2, 0, 1))
    slots_out = jnp.transpose(out_slots[0], (2, 0, 1))
    sends = jnp.transpose(send_lists[0, 0])
    ext = ZERO + 1
    half = gd.rows_pad // 2
    dma = pltpu.SemaphoreType.DMA
    block = (BLOCK, 128)
    slots = (MAP_CAP, 1, KERNEL)
    hbm, vmem = pl.BlockSpec(memory_space=pltpu.HBM), pl.BlockSpec(memory_space=pltpu.VMEM)
    flops = 2 * 128 ** 3 * KERNEL * 2 * (ZERO + MAP_CAP)
    grad, weight = pl.pallas_call(
        functools.partial(kernel, gd),
        out_shape=(
            jax.ShapeDtypeStruct((BLOCKS,) + block, F32),
            jax.ShapeDtypeStruct((gd.columns, gd.rows), F32),
        ),
        in_specs=[hbm] * 8,
        out_specs=(hbm, vmem),
        scratch_shapes=[
            pltpu.VMEM(slots, jnp.int32),
            pltpu.VMEM(slots, jnp.int32),
            pltpu.VMEM((32, 128), jnp.int32),
            pltpu.SMEM(slots, jnp.int32),
            pltpu.SMEM(slots, jnp.int32),
            pltpu.SMEM((SEND_CAP, 8), jnp.int32),
            pltpu.SMEM((32, 128), jnp.int32),
            pltpu.VMEM((BLOCKS,) + block, BF16),
            pltpu.VMEM((BLOCKS,) + block, BF16),
            pltpu.VMEM((KERNEL,) + block, BF16),
            pltpu.VMEM((KERNEL,) + block, BF16),
            pltpu.VMEM((BLOCKS,) + block, F32),
            pltpu.VMEM((BLOCKS,) + block, BF16),
            pltpu.VMEM((ext,) + block, BF16),
            pltpu.VMEM((ext,) + block, BF16),
            pltpu.VMEM((BLOCKS + 1,) + block, BF16),
            pltpu.VMEM((BLOCKS + 1,) + block, BF16),
            pltpu.VMEM((BLOCKS + 1,) + block, BF16),
            pltpu.VMEM((BLOCKS,) + block, F32),
            pltpu.VMEM((HALO,) + block, BF16),
            pltpu.VMEM((HALO,) + block, BF16),
            pltpu.VMEM((2, HALO) + block, BF16),
            pltpu.VMEM((HALO + 1,) + block, BF16),
            pltpu.VMEM((HALO + 1,) + block, BF16),
            pltpu.VMEM((2, SIDE) + block, BF16),
            pltpu.VMEM((2, SIDE) + block, BF16),
            pltpu.VMEM((SIDE,) + block, F32),
            pltpu.VMEM((2, gd.x_lo, gd.ring, SIDE // 2, 2 * gd.columns, 128), BF16),
            pltpu.VMEM((2, gd.x_lo, gd.ring, SIDE // 2, 2 * gd.columns, 128), BF16),
            pltpu.VMEM((SIDE // 2, 2 * gd.columns, 128), F32),
            pltpu.VMEM((2, gd.x_lo * gd.quarter, 2 * gd.columns, half), BF16),
            pltpu.VMEM((gd.sources, 2 * gd.columns, half), BF16),
            dma((13,)),
            dma((4, 8)),
            dma((4, 8)),
            dma((2,)),
            dma((2,)),
            dma((2, gd.x_lo, gd.ring)),
            dma((2, gd.x_lo, gd.ring)),
            dma((2, gd.x_lo * gd.quarter)),
            dma((gd.sources,)),
        ],
        compiler_params=pltpu.CompilerParams(
            collective_id=0, has_side_effects=True, vmem_limit_bytes=56 * 1024 * 1024
        ),
        cost_estimate=pl.CostEstimate(flops=flops, bytes_accessed=8 * 2 ** 20, transcendentals=0),
    )(slots_in, slots_out, sends, features_in[0, 0], pre_act[0, 0], cotangent[0, 0], w_first, w_second)
    weight = weight.T * (1.0 / math.sqrt(MAP_CAP * BLOCK * gd.n_gx * gd.n_gy))
    return grad.astype(BF16)[None, None], weight


def build(mesh, x_lo, x_hi):
    grid = Grid(mesh.shape["gx"], mesh.shape["gy"], x_lo, x_hi)
    in_specs = (
        P("gx", "gy", None, None, None),
        P("gx", "gy", None, None, None),
        P("gx", "gy", None, None, None),
        P(),
        P(),
        P("gx", "gy", None, None),
        P("gx", "gy", None, None),
        P("gx", "gy", None, None),
    )
    out_specs = (P("gx", "gy", None, None, None), P("gy", "gx"))
    return jax.shard_map(
        functools.partial(per_device, grid), mesh=mesh, in_specs=in_specs, out_specs=out_specs, check_vma=False
    )


def solution(mesh):
    return build(mesh, 2, 2)
```
